32 devices in a mesh: group: 2 (over core), seq: 4 (over z), tensor: 4 (over y, x).
Axes of the slice: x: 2, y: 2, z: 4, core: 2. Of those that a mesh axis runs over, the one named last changes fastest.
Arguments:
- prompt_hidden: bfloat16 [12288, 12288], P(('group', 'seq'), 'tensor')
- decode_hidden: bfloat16 [2, 32, 12288], P(None, ('group', 'seq'), 'tensor')
- norm_gain: bfloat16 [12288], P('tensor'), may hold values from 0.099609375 to 1.8984375
- kv_weight: bfloat16 [12288, 2048], P('tensor'), may hold values from -0.0546875 to 0.0546875
- kv_cache: bfloat16 [32, 8, 1024, 256], P(('group', 'seq'), None, 'tensor'), as said below
- queries: bfloat16 [2, 32, 12288], P(None, ('group', 'seq')), as said below
- lengths: int32 [32], replicated, may hold values from 2 to 254, as said below
- prompt_row: int32 [16], replicated, may hold values from 0 to 31, as said below
Outputs:
- decode_out: bfloat16 [2, 32, 12288], P(None, ('group', 'seq'), 'tensor')
The draws below stay inside these ranges and needn't reach their ends.
Inputs may be any that keep to these rules, and one draw needn't show every extreme that they name: `lengths`: one row has exactly 254 and one row exactly 2. `prompt_row`: no two prompts share a row. `kv_cache`: keys already rotated to their positions. queries already rotated to their positions.
All inputs are finite; a program needn't handle non-finite values.
Results may differ from the reference program's by a relative error of at most 0.02.
Values may be sent and summed in bfloat16 or wider, within the bound.
A program may use at most 128 MiB of HBM per device.

```python
import math
import jax
import jax.numpy as jnp
from jax import lax

D = 12288
KVH = 8
QH = 96
HD = 128
PLEN = 768
STEPS = 2
PTOKENS = 12288
PROMPTS = 16
ROWS = 32
CACHE = 1024
MAXLEN = 254


def scale_table(key, full_shape, upper_scale):
    row_key, column_key = jax.random.split(key)
    columns = full_shape[-1]
    row_scale = jnp.exp(jax.random.uniform(row_key, full_shape[:-1] + (1,), jnp.float32, 0.0, math.log(upper_scale)))
    rising = jnp.exp(jnp.arange(columns, dtype=jnp.float32) * (math.log(3.0) / columns))
    column_scale = rising * jnp.exp(jax.random.uniform(column_key, (columns,), jnp.float32, 0.0, math.log(upper_scale)))
    return row_scale * column_scale


def anchor_keys(key):
    return jax.random.normal(jax.random.fold_in(key, 71), (ROWS, KVH, HD), jnp.float32)


def draw_prompt_hidden(key, part):
    key = jax.random.fold_in(key, 11)
    noise_key, scale_key = jax.random.split(key, 2)
    full_shape = (PTOKENS, D)
    noise_part = jax.random.normal(noise_key, full_shape, jnp.float32)
    return (noise_part * scale_table(scale_key, full_shape, 10.0)).astype(jnp.bfloat16)


def draw_decode_hidden(key, part):
    key = jax.random.fold_in(key, 16)
    noise_key, scale_key = jax.random.split(key, 2)
    full_shape = (STEPS, ROWS, D)
    noise_part = jax.random.normal(noise_key, full_shape, jnp.float32)
    return (noise_part * scale_table(scale_key, full_shape, 10.0)).astype(jnp.bfloat16)


def draw_kv_cache(key, part):
    anchor = anchor_keys(key)
    key = jax.random.fold_in(key, 12)
    full_shape = (ROWS, KVH, CACHE, 2 * HD)
    cache_draw = jax.random.normal(key, full_shape, jnp.float32)
    cache_draw = cache_draw.at[:, :, 0, :HD].set(anchor)
    return cache_draw.astype(jnp.bfloat16)


def draw_queries(key, part):
    key = jax.random.fold_in(key, 13)
    full_shape = (STEPS, ROWS, QH * HD)
    return (2.5 * jax.random.normal(key, full_shape, jnp.float32)).astype(jnp.bfloat16)


def draw_lengths(key, part):
    key = jax.random.fold_in(key, 14)
    raw_key, order_key = jax.random.split(key)
    raw_draw = jax.random.randint(raw_key, (ROWS,), 0, 1024)
    spread = 2 + (MAXLEN - 2) * (raw_draw * raw_draw // 1024) // 1024
    row_order = jax.random.permutation(order_key, ROWS)
    row_index = jnp.arange(ROWS, dtype=jnp.int32)
    spread = jnp.where(row_index == row_order[0], MAXLEN, spread)
    spread = jnp.where(row_index == row_order[1], 2, spread)
    return spread.astype(jnp.int32)


def draw_prompt_row(key, part):
    key = jax.random.fold_in(key, 15)
    middle_key, order_key = jax.random.split(key)
    middle = 1 + jax.random.permutation(middle_key, ROWS - 2)[:PROMPTS - 2]
    chosen = jnp.concatenate([jnp.array([0, ROWS - 1], jnp.int32), middle.astype(jnp.int32)])
    return jax.random.permutation(order_key, chosen).astype(jnp.int32)


def level_of(stream_key, dims, shards, low, high):
    gain = 1.0
    for position, shards_of in shards:
        steps = jax.random.uniform(jax.random.fold_in(jax.random.fold_in(stream_key, 6), position), (shards_of,), jnp.float32, low / len(shards), high / len(shards))
        gain = gain * jnp.repeat(jnp.exp(steps), dims[position] // shards_of).reshape((-1,) + (1,) * (len(dims) - 1 - position))
    return gain


def noise(key, dims, width, reach, pieces=(), held_as=jnp.bfloat16):
    result = jax.random.normal(key, dims, jnp.float32) * width
    if len(pieces) > 0:
        result = level_of(key, dims, pieces, -0.22, 0.18) * result
    return jnp.clip(result, min=-reach, max=reach).astype(held_as)


def setup_inputs(seed: int = 0) -> dict:
    seeds = jax.random.split(jax.random.key(seed), 9)
    return {
        "prompt_hidden": draw_prompt_hidden(jax.random.fold_in(seeds[8], 71), 0),
        "decode_hidden": draw_decode_hidden(jax.random.fold_in(seeds[8], 71), 0),
        "norm_gain": jnp.clip(1.0 + 0.18 * jax.random.normal(seeds[2], (D,), jnp.float32), 0.099609375, 1.8984375).astype(jnp.bfloat16),
        "kv_weight": noise(seeds[3], (D, 2 * KVH * HD), D ** -0.5, 0.0546875, ((0, 4),)),
        "kv_cache": draw_kv_cache(jax.random.fold_in(seeds[8], 71), 0),
        "queries": draw_queries(jax.random.fold_in(seeds[8], 71), 0),
        "lengths": draw_lengths(jax.random.fold_in(seeds[8], 71), 0),
        "prompt_row": draw_prompt_row(jax.random.fold_in(seeds[8], 71), 0),
    }


epsilon = 1e-05
rope_base = 1000000.0
very_negative = -1e+30

def rotate(values, positions):
    halfway = values.shape[-1] // 2
    exponents = jnp.arange(halfway, dtype=jnp.float32) * (-2.0 / values.shape[-1])
    frequency = jnp.power(rope_base, exponents)
    angles = positions.astype(jnp.float32)[..., None] * frequency
    cosine = jnp.cos(angles)
    sine_part = jnp.sin(angles)
    leading = values[..., :halfway]
    trailing = values[..., halfway:]
    return jnp.concatenate([leading * cosine - trailing * sine_part, trailing * cosine + leading * sine_part], -1)

def project(hidden, norm_gain, kv_weight):
    hidden_wide = hidden.astype(jnp.float32)
    mean_square = lax.optimization_barrier(jnp.mean(hidden_wide * hidden_wide, axis=-1))
    weighted = (hidden_wide * norm_gain.astype(jnp.float32)).astype(jnp.bfloat16)
    projected = jnp.dot(weighted, kv_weight, preferred_element_type=jnp.float32)
    return projected * lax.rsqrt(mean_square + epsilon)[:, None]

def split_heads(projected, positions):
    head_parts = projected.reshape(projected.shape[0], KVH, 2, HD)
    key_part = rotate(head_parts[:, :, 0], positions[:, None]).astype(jnp.bfloat16)
    value_part = head_parts[:, :, 1].astype(jnp.bfloat16)
    return (lax.optimization_barrier(key_part), lax.optimization_barrier(value_part))

def reference(prompt_hidden, decode_hidden, norm_gain, kv_weight, kv_cache, queries, lengths, prompt_row):
    token_index = jnp.arange(PTOKENS, dtype=jnp.int32)
    owner_row = prompt_row[token_index // PLEN]
    prompt_pos = lengths[owner_row] + token_index % PLEN
    prompt_keys, prompt_values = split_heads(project(prompt_hidden, norm_gain, kv_weight), prompt_pos)
    row_ids = jnp.arange(ROWS, dtype=jnp.int32)
    is_new = jnp.any(prompt_row[None, :] == row_ids[:, None], axis=1)
    step_pos = lengths[None, :] + PLEN * is_new.astype(jnp.int32)[None, :] + jnp.arange(STEPS, dtype=jnp.int32)[:, None]
    step_keys, step_values = split_heads(project(decode_hidden.reshape(STEPS * ROWS, D), norm_gain, kv_weight), step_pos.reshape(-1))
    step_keys = step_keys.reshape(STEPS, ROWS, KVH, HD)
    step_values = step_values.reshape(STEPS, ROWS, KVH, HD)
    prompt_ids = jnp.arange(PROMPTS, dtype=jnp.int32)
    prompt_of_row = lax.optimization_barrier(jnp.sum(jnp.where(prompt_row[None, :] == row_ids[:, None], prompt_ids[None, :], 0), axis=1))
    score_scale = 1.0 / math.sqrt(HD)
    step_ids = jnp.arange(STEPS, dtype=jnp.int32)

    def attend(row_index):
        query_rows = queries[:, row_index].astype(jnp.float32).reshape(STEPS, KVH, QH // KVH, HD)
        cache_row = kv_cache[row_index]
        first_token = (prompt_of_row[row_index] * PLEN).astype(jnp.int32)
        new_keys = lax.dynamic_slice_in_dim(prompt_keys, first_token, PLEN, 0)
        new_values = lax.dynamic_slice_in_dim(prompt_values, first_token, PLEN, 0)
        all_keys = jnp.concatenate([cache_row[:, :, :HD], jnp.transpose(new_keys, (1, 0, 2)), jnp.transpose(step_keys[:, row_index], (1, 0, 2))], axis=1)
        all_values = jnp.concatenate([cache_row[:, :, HD:], jnp.transpose(new_values, (1, 0, 2)), jnp.transpose(step_values[:, row_index], (1, 0, 2))], axis=1)
        cache_mask = jnp.broadcast_to((jnp.arange(CACHE, dtype=jnp.int32) < lengths[row_index])[None, :], (STEPS, CACHE))
        new_mask = jnp.broadcast_to(is_new[row_index], (STEPS, PLEN))
        own_mask = step_ids[None, :] <= step_ids[:, None]
        full_mask = jnp.concatenate([cache_mask, new_mask, own_mask], axis=1)[:, None, None, :]
        scores = jnp.einsum('sgqd,gld->sgql', query_rows, all_keys.astype(jnp.float32)) * score_scale
        masked = jnp.where(full_mask, scores, very_negative)
        row_top = lax.optimization_barrier(jnp.max(masked, axis=-1, keepdims=True))
        weights = jnp.where(full_mask, jnp.exp(masked - row_top), 0.0)
        weight_total = lax.optimization_barrier(jnp.sum(weights, axis=-1))
        rounded = lax.optimization_barrier(weights.astype(jnp.bfloat16)).astype(jnp.float32)
        mixed_sum = jnp.einsum('sgql,gld->sgqd', rounded, all_values.astype(jnp.float32))
        return (mixed_sum / weight_total[..., None]).reshape(STEPS, QH * HD).astype(jnp.bfloat16)
    outputs = lax.map(attend, row_ids)
    return jnp.transpose(outputs, (1, 0, 2))
```

```python
import math

import jax
import jax.numpy as jnp
from jax import lax
from jax.sharding import PartitionSpec as P

D = 12288
PLEN = 768


epsilon = 1e-05
rope_base = 1000000.0
very_negative = -1e30


def angle_parts(positions, head_size):
    halfway = head_size // 2
    exponents = jnp.arange(halfway, dtype=jnp.float32) * (-2.0 / head_size)
    frequency = jnp.power(rope_base, exponents)
    angles = positions.astype(jnp.float32)[..., None] * frequency
    return jnp.cos(angles), jnp.sin(angles)


def rotate(values, cosine, sine_part):
    halfway = values.shape[-1] // 2
    leading = values[..., :halfway]
    trailing = values[..., halfway:]
    return jnp.concatenate(
        [leading * cosine - trailing * sine_part, trailing * cosine + leading * sine_part], -1
    )


def per_device(
    prompt_hidden, decode_hidden, norm_gain, kv_weight, kv_cache, queries, lengths, prompt_row
):
    shards = ("group", "seq")
    tensor_count = lax.axis_size("tensor")
    tensor_rank = lax.axis_index("tensor")
    shard_rank = lax.axis_index(shards)
    token_count, features = prompt_hidden.shape
    steps_count, row_count, query_width = queries.shape
    kv_heads = kv_cache.shape[1]
    cache_rows = kv_cache.shape[2]
    head_size = kv_cache.shape[3] // 2
    query_heads = query_width // head_size
    group_size = query_heads // kv_heads
    local_heads = query_heads // tensor_count
    local_prompts = token_count // PLEN
    score_scale = 1.0 / math.sqrt(head_size)
    row_total = lengths.shape[0]

    my_owners = lax.dynamic_slice_in_dim(
        prompt_row, shard_rank * local_prompts, local_prompts, 0
    )
    width = query_width // tensor_count
    my_queries = lax.dynamic_slice_in_dim(queries, tensor_rank * width, width, 2)
    query_rows = lax.all_gather(my_queries, shards, axis=1, tiled=True)
    owner_queries = jnp.take(query_rows, my_owners, axis=1)
    owner_queries = lax.all_gather(owner_queries, "tensor", axis=2, tiled=True)
    owner_queries = owner_queries.reshape(
        steps_count, local_prompts, kv_heads, group_size, head_size
    )

    gain_wide = norm_gain.astype(jnp.float32)
    prompt_wide = prompt_hidden.astype(jnp.float32)
    prompt_square = jnp.sum(prompt_wide * prompt_wide, axis=1)
    prompt_weighted = (prompt_wide * gain_wide).astype(jnp.bfloat16)
    decode_wide = decode_hidden.astype(jnp.float32)
    decode_square = jnp.sum(decode_wide * decode_wide, axis=2)
    decode_weighted = (decode_wide * gain_wide).astype(jnp.bfloat16)
    decode_terms = jnp.einsum(
        "srk,kc->src", decode_weighted, kv_weight, preferred_element_type=jnp.float32
    )

    my_rows = shard_rank * row_count + jnp.arange(row_count, dtype=jnp.int32)
    my_lengths = lax.dynamic_slice_in_dim(lengths, shard_rank * row_count, row_count, 0)
    query_blocks = queries.reshape(steps_count, row_count, kv_heads, group_size, head_size)
    cache_pos = tensor_rank * cache_rows + jnp.arange(cache_rows, dtype=jnp.int32)
    cache_mask = (cache_pos[None, :] < my_lengths[:, None])[:, None, None, None, :]
    cache_scores = (
        jnp.einsum(
            "srgqd,rgpd->rgsqp",
            query_blocks,
            kv_cache[..., :head_size],
            preferred_element_type=jnp.float32,
        )
        * score_scale
    )
    cache_scores = jnp.where(cache_mask, cache_scores, very_negative)
    cache_top = jnp.max(cache_scores, axis=-1)
    cache_top = lax.pmax(cache_top, "tensor")
    cache_weights = jnp.where(cache_mask, jnp.exp(cache_scores - cache_top[..., None]), 0.0)
    cache_total = jnp.sum(cache_weights, axis=-1)
    cache_mixed = jnp.einsum(
        "rgsqp,rgpd->gqsrd",
        cache_weights.astype(jnp.bfloat16),
        kv_cache[..., head_size:],
        preferred_element_type=jnp.float32,
    ).reshape(query_heads, steps_count, row_count, head_size)
    cache_mixed = lax.psum_scatter(cache_mixed, "tensor", scatter_dimension=0, tiled=True)

    prompt_square, decode_square, decode_terms, cache_total = lax.psum(
        (prompt_square, decode_square, decode_terms, cache_total), "tensor"
    )

    weight_heads = kv_weight.reshape(features, kv_heads, 2, head_size)
    positions = (
        jnp.take(lengths, my_owners)[:, None] + jnp.arange(PLEN, dtype=jnp.int32)[None, :]
    )
    cosine, sine_part = angle_parts(positions, head_size)
    key_part = jnp.dot(
        prompt_weighted,
        weight_heads[:, :, 0].reshape(features, kv_heads * head_size),
        preferred_element_type=jnp.float32,
    ).reshape(local_prompts, PLEN, kv_heads, head_size)
    key_part = rotate(key_part, cosine[:, :, None], sine_part[:, :, None]).astype(jnp.bfloat16)
    scores = jnp.einsum(
        "spgqd,pngd->pgsqn", owner_queries, key_part, preferred_element_type=jnp.float32
    )
    scores = lax.psum(scores, "tensor")

    value_part = jnp.dot(
        prompt_weighted,
        weight_heads[:, :, 1].reshape(features, kv_heads * head_size),
        preferred_element_type=jnp.float32,
    ).astype(jnp.bfloat16)
    value_part = value_part.reshape(local_prompts, PLEN, kv_heads, head_size)

    factor = lax.rsqrt(prompt_square / D + epsilon).reshape(local_prompts, 1, 1, 1, PLEN)
    scores = scores * (factor * score_scale)
    prompt_top = jnp.max(scores, axis=-1)
    weights = jnp.exp(scores - prompt_top[..., None])
    prompt_total = jnp.sum(weights, axis=-1)
    prompt_log = prompt_top + jnp.log(prompt_total)
    mixed = jnp.einsum(
        "pgsqn,pngd->gqspd",
        (weights * factor).astype(jnp.bfloat16),
        value_part,
        preferred_element_type=jnp.float32,
    )
    totals = jnp.transpose(prompt_total, (1, 3, 2, 0))
    mixed = (mixed / totals[..., None]).reshape(
        query_heads, steps_count, local_prompts, head_size
    )
    mixed = lax.psum_scatter(mixed, "tensor", scatter_dimension=0, tiled=True)
    first_head = tensor_rank * local_heads
    prompt_log = jnp.transpose(prompt_log, (1, 3, 2, 0)).reshape(
        query_heads, steps_count, local_prompts
    )
    prompt_log = lax.dynamic_slice_in_dim(prompt_log, first_head, local_heads, 0)
    log_all = lax.all_gather(prompt_log, shards, axis=2, tiled=True)
    mixed_all = lax.all_gather(mixed.astype(jnp.bfloat16), shards, axis=2, tiled=True)

    owned = prompt_row[None, :] == my_rows[:, None]
    is_new = jnp.any(owned, axis=1)
    prompt_of_row = jnp.argmax(owned, axis=1)
    row_log = jnp.take(log_all, prompt_of_row, axis=2)
    row_log = jnp.where(is_new[None, None, :], row_log, very_negative)
    row_mixed = jnp.take(mixed_all, prompt_of_row, axis=2).astype(jnp.float32)
    row_mixed = jnp.where(is_new[None, None, :, None], row_mixed, 0.0)

    step_ids = jnp.arange(steps_count, dtype=jnp.int32)
    step_pos = my_lengths[None, :] + PLEN * is_new.astype(jnp.int32)[None, :] + step_ids[:, None]
    decode_scaled = decode_terms * lax.rsqrt(decode_square / D + epsilon)[..., None]
    decode_heads = decode_scaled.reshape(steps_count, row_count, kv_heads, 2, head_size)
    step_cosine, step_sine = angle_parts(step_pos, head_size)
    step_keys = rotate(
        decode_heads[:, :, :, 0], step_cosine[:, :, None], step_sine[:, :, None]
    ).astype(jnp.bfloat16)
    step_values = decode_heads[:, :, :, 1].astype(jnp.bfloat16)
    step_scores = (
        jnp.einsum(
            "srgqd,trgd->gqsrt", query_blocks, step_keys, preferred_element_type=jnp.float32
        )
        * score_scale
    )
    causal = step_ids[None, :] <= step_ids[:, None]
    step_mask = causal[None, None, :, None, :]
    step_scores = jnp.where(step_mask, step_scores, very_negative)
    step_top = jnp.max(step_scores, axis=-1)
    step_weights = jnp.where(step_mask, jnp.exp(step_scores - step_top[..., None]), 0.0)
    step_total = jnp.sum(step_weights, axis=-1)
    step_mixed = jnp.einsum(
        "gqsrt,trgd->gqsrd",
        step_weights.astype(jnp.bfloat16),
        step_values,
        preferred_element_type=jnp.float32,
    )

    def own(array):
        flat = array.reshape((query_heads,) + array.shape[2:])
        return lax.dynamic_slice_in_dim(flat, first_head, local_heads, 0)

    step_top, step_total, step_mixed = own(step_top), own(step_total), own(step_mixed)
    cache_top = own(jnp.transpose(cache_top, (1, 3, 2, 0)))
    cache_total = own(jnp.transpose(cache_total, (1, 3, 2, 0)))

    top = jnp.maximum(jnp.maximum(step_top, cache_top), row_log)
    step_factor = jnp.exp(step_top - top)
    cache_factor = jnp.exp(cache_top - top)
    row_factor = jnp.exp(row_log - top)
    total = step_total * step_factor + cache_total * cache_factor + row_factor
    result = (
        step_mixed * step_factor[..., None]
        + cache_mixed * cache_factor[..., None]
        + row_mixed * row_factor[..., None]
    ) / total[..., None]
    result = jnp.transpose(result, (1, 2, 0, 3)).reshape(
        steps_count, row_count, local_heads * head_size
    )
    return result.astype(jnp.bfloat16)


def solution(mesh):
    return jax.shard_map(
        per_device,
        mesh=mesh,
        in_specs=(
            P(("group", "seq"), "tensor"),
            P(None, ("group", "seq"), "tensor"),
            P("tensor"),
            P("tensor", None),
            P(("group", "seq"), None, "tensor", None),
            P(None, ("group", "seq"), None),
            P(),
            P(),
        ),
        out_specs=P(None, ("group", "seq"), "tensor"),
        check_vma=False,
    )
```

```python
import functools
import math

import jax
import jax.numpy as jnp
from jax import lax
from jax.experimental import pallas as pl
from jax.experimental.pallas import tpu as pltpu
from jax.sharding import PartitionSpec as P

D = 12288
PLEN = 768
BLOCK = 256
LANES = 128


epsilon = 1e-05
rope_base = 1000000.0
very_negative = -1e30
f32 = jnp.float32
bf16 = jnp.bfloat16
contract_last = (((1,), (1,)), ((), ()))
contract_inner = (((1,), (0,)), ((), ()))


def angle_tables(positions, head_size):
    halfway = head_size // 2
    exponents = jnp.arange(halfway, dtype=f32) * (-2.0 / head_size)
    frequency = jnp.power(rope_base, exponents)
    angles = positions.astype(f32)[..., None] * frequency
    cosine, sine_part = jnp.cos(angles), jnp.sin(angles)
    return (
        jnp.concatenate([cosine, cosine], -1),
        jnp.concatenate([-sine_part, sine_part], -1),
    )


def rotated(values, cosine, sine_part):
    return values * cosine + pltpu.roll(values, values.shape[-1] // 2, 1) * sine_part


def kernel(
    sizes,
    prompt_ref,
    step_hidden_ref,
    gain_ref,
    weight_ref,
    cache_ref,
    query_ref,
    cos_ref,
    sin_ref,
    step_cos_ref,
    step_sin_ref,
    owner_ref,
    length_ref,
    new_ref,
    pick_ref,
    out_ref,
    xw,
    wk,
    wv,
    cbuf,
    acc,
    kbuf,
    vbuf,
    q1,
    q2,
    sq,
    sqd,
    s_send,
    s_recv,
    w_all,
    lse_all,
    linv,
    o_send,
    o_recv,
    o_all,
    c_send,
    c_recv,
    cl_send,
    cl_recv,
    d_send,
    d_recv,
    x_sem,
    w_sem,
    c_sem,
    shard_sems,
    tensor_sems,
):
    n_t, n_s, n_seq, kpc, unit, group, steps, rows = sizes
    tokens, features = prompt_ref.shape
    prompts = tokens // PLEN
    cache_rows = cbuf.shape[2]
    me = lax.axis_index("tensor")
    my_seq = lax.axis_index("seq")
    shard = lax.axis_index("group") * n_seq + my_seq
    scale = 1.0 / math.sqrt(LANES)
    unit_rows = unit * steps

    def chunk(k):
        return lax.rem(me + 1 + k, n_t)

    def head_of(t, j):
        return (t * kpc * unit + j * unit) // group

    def to_tensor(src, dst, which, k):
        return pltpu.make_async_remote_copy(
            src_ref=src,
            dst_ref=dst,
            send_sem=tensor_sems.at[which, 0, k],
            recv_sem=tensor_sems.at[which, 1, k],
            device_id={"tensor": chunk(k)},
            device_id_type=pl.DeviceIdType.MESH,
        )

    def to_shard(src, dst, which, k):
        peer = lax.rem(shard + 1 + k, n_s)
        return pltpu.make_async_remote_copy(
            src_ref=src,
            dst_ref=dst,
            send_sem=shard_sems.at[which, 0, k],
            recv_sem=shard_sems.at[which, 1, k],
            device_id={"group": peer // n_seq, "seq": lax.rem(peer, n_seq)},
            device_id_type=pl.DeviceIdType.MESH,
        )

    def each(count, body):
        def step(k, carry):
            body(k)
            return carry

        lax.fori_loop(0, count, step, 0)

    def gather(maker, ref, mine, which, count):
        each(count, lambda k: maker(ref.at[mine], ref.at[mine], which, k).start())

    def gathered(maker, ref, mine, which, count, total):
        def body(k):
            source = lax.rem(mine - 1 - k + total, total)
            maker(ref.at[mine], ref.at[source], which, k).wait_recv()

        each(count, body)

    def sent(maker, ref, mine, which, count):
        each(count, lambda k: maker(ref.at[mine], ref.at[mine], which, k).wait_send())

    blocks = tokens // BLOCK

    def x_copy(b):
        at = pl.ds(pl.multiple_of(b * BLOCK, BLOCK), BLOCK)
        return pltpu.make_async_copy(prompt_ref.at[at], xw.at[at], x_sem.at[b])

    def w_copy(k, j, value):
        column = pl.multiple_of(head_of(chunk(k), j) * 2 * LANES + value * LANES, LANES)
        dst = (wv if value else wk).at[k, :, pl.ds(j * LANES, LANES)]
        return pltpu.make_async_copy(
            weight_ref.at[:, pl.ds(column, LANES)], dst, w_sem.at[value, j, k]
        )

    c_copy = pltpu.make_async_copy(cache_ref, cbuf, c_sem)
    each(blocks, lambda b: x_copy(b).start())
    for value in range(2):
        for j in range(kpc):
            each(n_t, lambda k: w_copy(k, j, value).start())
    c_copy.start()

    barrier = pltpu.get_barrier_semaphore()

    def greet_tensor(k):
        pl.semaphore_signal(
            barrier, inc=1, device_id={"tensor": chunk(k)}, device_id_type=pl.DeviceIdType.MESH
        )

    def greet_shard(k):
        peer = lax.rem(shard + 1 + k, n_s)
        pl.semaphore_signal(
            barrier,
            inc=1,
            device_id={"group": peer // n_seq, "seq": lax.rem(peer, n_seq)},
            device_id_type=pl.DeviceIdType.MESH,
        )

    each(n_t - 1, greet_tensor)
    each(n_s - 1, greet_shard)
    pl.semaphore_wait(barrier, n_t + n_s - 2)

    q1[shard] = query_ref[me]
    gather(to_shard, q1, shard, 0, n_s - 1)

    def weigh(b):
        x_copy(b).wait()
        at = pl.ds(pl.multiple_of(b * BLOCK, BLOCK), BLOCK)
        square = jnp.zeros((BLOCK, LANES), f32)
        for c in range(features // LANES):
            lanes = pl.ds(c * LANES, LANES)
            wide = xw[at, lanes].astype(f32)
            square += wide * wide
            xw[at, lanes] = (wide * gain_ref[:, lanes].astype(f32)).astype(bf16)
        total = jnp.sum(square.T, axis=0, keepdims=True)
        sq[me, b] = jnp.broadcast_to(total, (8, BLOCK))

    each(blocks, weigh)
    wide = step_hidden_ref[...].astype(f32)
    sqd[me] = jnp.broadcast_to(
        jnp.sum(wide * wide, axis=1, keepdims=True), (wide.shape[0], LANES)
    )
    pad = wide.shape[0]
    xw[pl.ds(tokens, pad), :] = (wide * gain_ref[...].astype(f32)).astype(bf16)
    gather(to_tensor, sq, me, 0, n_t - 1)
    gather(to_tensor, sqd, me, 1, n_t - 1)

    def keys(k):
        for j in range(kpc):
            w_copy(k, j, 0).wait()
        acc[...] = jnp.dot(xw[...], wk[k], preferred_element_type=f32)
        for j in range(kpc):
            lanes = pl.ds(j * LANES, LANES)
            for p in range(prompts):
                part = acc[pl.ds(p * PLEN, PLEN), lanes]
                kbuf[k, p, j] = rotated(part, cos_ref[p], sin_ref[p]).astype(bf16)
            d_send[k, 0, j] = acc[pl.ds(tokens, pad), lanes]

    each(n_t, keys)

    gathered(to_shard, q1, shard, 0, n_s - 1, n_s)
    for p in range(prompts):
        owner = owner_ref[p]
        q2[me, p] = q1[owner // rows, lax.rem(owner, rows)]
    gather(to_tensor, q2, me, 2, n_t - 1)
    gathered(to_tensor, q2, me, 2, n_t - 1, n_t)

    def score(k):
        t = chunk(k)
        for p in range(prompts):
            for j in range(kpc):
                s_send[k, p, j] = lax.dot_general(
                    q2[t, p, j], kbuf[k, p, j], contract_last, preferred_element_type=f32
                )

        @pl.when(k < n_t - 1)
        def _():
            to_tensor(s_send.at[k], s_recv.at[k], 3, k).start()

    each(n_t, score)

    def values(k):
        for j in range(kpc):
            w_copy(k, j, 1).wait()
        acc[...] = jnp.dot(xw[...], wv[k], preferred_element_type=f32)
        for j in range(kpc):
            lanes = pl.ds(j * LANES, LANES)
            for p in range(prompts):
                vbuf[k, p, j] = acc[pl.ds(p * PLEN, PLEN), lanes].astype(bf16)
            d_send[k, 1, j] = acc[pl.ds(tokens, pad), lanes]

        @pl.when(k < n_t - 1)
        def _():
            to_tensor(d_send.at[k], d_recv.at[k], 4, k).start()

    each(n_t, values)

    c_copy.wait()
    position = me * cache_rows + lax.broadcasted_iota(jnp.int32, (unit_rows, cache_rows), 1)
    lane = lax.broadcasted_iota(jnp.int32, (unit_rows, LANES), 1)
    per_row = LANES // rows

    def resident(k):
        t = chunk(k)
        for j in range(kpc):
            g = head_of(t, j)
            packed = jnp.zeros((unit_rows, LANES), f32)
            for r in range(rows):
                found = lax.dot_general(
                    query_ref[t, r, j],
                    cbuf[r, g, :, pl.ds(0, LANES)],
                    contract_last,
                    preferred_element_type=f32,
                )
                mask = position < length_ref[r]
                found = jnp.where(mask, found * scale, very_negative)
                top = jnp.max(found, axis=1, keepdims=True)
                weights = jnp.where(mask, jnp.exp(found - top), 0.0)
                total = jnp.sum(weights, axis=1, keepdims=True)
                some = total > 0.0
                total = jnp.where(some, total, 1.0)
                mixed = lax.dot_general(
                    weights.astype(bf16),
                    cbuf[r, g, :, pl.ds(LANES, LANES)],
                    contract_inner,
                    preferred_element_type=f32,
                )
                c_send[k, r, j] = (mixed / total).astype(bf16)
                log = jnp.where(some, top + jnp.log(total), very_negative)
                packed = jnp.where(lane // per_row == r, log, packed)
            cl_send[k, j] = packed

        @pl.when(k < n_t - 1)
        def _():
            to_tensor(c_send.at[k], c_recv.at[k], 5, k).start()
            to_tensor(cl_send.at[k], cl_recv.at[k], 6, k).start()

    each(n_t, resident)

    gathered(to_tensor, sq, me, 0, n_t - 1, n_t)
    gathered(to_tensor, sqd, me, 1, n_t - 1, n_t)
    each(n_t - 1, lambda k: to_tensor(s_send.at[k], s_recv.at[k], 3, k).wait_recv())
    per_prompt = PLEN // BLOCK
    for p in range(prompts):
        parts = []
        for b in range(per_prompt):
            total = sq[0, p * per_prompt + b]
            for t in range(1, n_t):
                total += sq[t, p * per_prompt + b]
            parts.append(lax.rsqrt(total[0:1] / D + epsilon))
        factor = jnp.concatenate(parts, axis=1)
        for j in range(kpc):
            total = s_send[n_t - 1, p, j]
            for k in range(n_t - 1):
                total += s_recv[k, p, j]
            total = total * (factor * scale)
            top = jnp.max(total, axis=1, keepdims=True)
            weights = jnp.exp(total - top)
            whole = jnp.sum(weights, axis=1, keepdims=True)
            w_all[me, p, j] = (weights * factor).astype(bf16)
            lse_all[shard, p, j] = jnp.broadcast_to(top + jnp.log(whole), (unit_rows, LANES))
            linv[p, j] = jnp.broadcast_to(1.0 / whole, (unit_rows, LANES))
    gather(to_tensor, w_all, me, 7, n_t - 1)
    gather(to_shard, lse_all, shard, 1, n_s - 1)

    def mix(k):
        t = chunk(k)

        @pl.when(k < n_t - 1)
        def _():
            to_tensor(w_all.at[me], w_all.at[t], 7, n_t - 2 - k).wait_recv()

        for p in range(prompts):
            for j in range(kpc):
                o_send[k, p, j] = lax.dot_general(
                    w_all[t, p, j], vbuf[k, p, j], contract_inner, preferred_element_type=f32
                )

        @pl.when(k < n_t - 1)
        def _():
            to_tensor(o_send.at[k], o_recv.at[k], 8, k).start()

    each(n_t, mix)
    each(n_t - 1, lambda k: to_tensor(o_send.at[k], o_recv.at[k], 8, k).wait_recv())
    for p in range(prompts):
        for j in range(kpc):
            total = o_send[n_t - 1, p, j]
            for k in range(n_t - 1):
                total += o_recv[k, p, j]
            o_all[shard, p, j] = (total * linv[p, j]).astype(bf16)
    gather(to_shard, o_all, shard, 2, n_s - 1)

    each(n_t - 1, lambda k: to_tensor(d_send.at[k], d_recv.at[k], 4, k).wait_recv())
    each(n_t - 1, lambda k: to_tensor(c_send.at[k], c_recv.at[k], 5, k).wait_recv())
    each(n_t - 1, lambda k: to_tensor(cl_send.at[k], cl_recv.at[k], 6, k).wait_recv())
    total = sqd[0]
    for t in range(1, n_t):
        total += sqd[t]
    factor = lax.rsqrt(total / D + epsilon)
    own_row = lax.broadcasted_iota(jnp.int32, (unit_rows, pad), 0)
    column = lax.broadcasted_iota(jnp.int32, (unit_rows, pad), 1)
    causal = (column // rows <= own_row // unit) & (column < steps * rows)
    states = {}
    for j in range(kpc):
        terms = []
        for value in range(2):
            total = d_send[n_t - 1, value, j]
            for k in range(n_t - 1):
                total += d_recv[k, value, j]
            terms.append(total * factor)
        key = rotated(terms[0], step_cos_ref[...], step_sin_ref[...]).astype(bf16)
        value = terms[1].astype(bf16)
        for r in range(rows):
            found = lax.dot_general(
                query_ref[me, r, j], key, contract_last, preferred_element_type=f32
            )
            mask = causal & (lax.rem(column, rows) == r)
            found = jnp.where(mask, found * scale, very_negative)
            top = jnp.max(found, axis=1, keepdims=True)
            logs = [cl_send[n_t - 1, j][:, r * per_row : r * per_row + 1]]
            outs = [c_send[n_t - 1, r, j]]
            for k in range(n_t - 1):
                logs.append(cl_recv[k, j][:, r * per_row : r * per_row + 1])
                outs.append(c_recv[k, r, j])
            for log in logs:
                top = jnp.maximum(top, log)
            weights = jnp.where(mask, jnp.exp(found - top), 0.0)
            whole = jnp.sum(weights, axis=1, keepdims=True)
            mixed = lax.dot_general(
                weights.astype(bf16), value, contract_inner, preferred_element_type=f32
            )
            for log, out in zip(logs, outs):
                share = jnp.exp(log - top)
                whole += share
                mixed += share * out.astype(f32)
            states[j, r] = (top, whole, mixed)

    gathered(to_shard, lse_all, shard, 1, n_s - 1, n_s)
    gathered(to_shard, o_all, shard, 2, n_s - 1, n_s)
    for j in range(kpc):
        for r in range(rows):
            top, whole, mixed = states[j, r]
            pick = pick_ref[r]
            source, p = pick // prompts, lax.rem(pick, prompts)
            log = lse_all[source, p, j]
            log = jnp.where(new_ref[r] > 0, log, very_negative)
            out = o_all[source, p, j].astype(f32)
            last = jnp.maximum(top, log)
            left, right = jnp.exp(top - last), jnp.exp(log - last)
            out_ref[r, j] = ((mixed * left + out * right) / (whole * left + right)).astype(bf16)

    sent(to_shard, q1, shard, 0, n_s - 1)
    sent(to_shard, lse_all, shard, 1, n_s - 1)
    sent(to_shard, o_all, shard, 2, n_s - 1)
    sent(to_tensor, sq, me, 0, n_t - 1)
    sent(to_tensor, sqd, me, 1, n_t - 1)
    sent(to_tensor, q2, me, 2, n_t - 1)
    sent(to_tensor, w_all, me, 7, n_t - 1)
    for which, src, dst in (
        (3, s_send, s_recv),
        (4, d_send, d_recv),
        (5, c_send, c_recv),
        (6, cl_send, cl_recv),
        (8, o_send, o_recv),
    ):
        each(n_t - 1, lambda k: to_tensor(src.at[k], dst.at[k], which, k).wait_send())


def per_device(
    prompt_hidden, decode_hidden, norm_gain, kv_weight, kv_cache, queries, lengths, prompt_row
):
    shards = ("group", "seq")
    n_t = lax.axis_size("tensor")
    n_s = lax.axis_size(shards)
    n_seq = lax.axis_size("seq")
    shard_rank = lax.axis_index(shards)
    tokens, features = prompt_hidden.shape
    steps, rows, query_width = queries.shape
    kv_heads, cache_rows = kv_cache.shape[1:3]
    head_size = kv_cache.shape[3] // 2
    query_heads = query_width // head_size
    group = query_heads // kv_heads
    local_heads = query_heads // n_t
    unit = min(local_heads, group)
    kpc = local_heads // unit
    prompts = tokens // PLEN
    unit_rows = unit * steps
    pad = -(-steps * rows // 16) * 16
    cols = kpc * head_size

    my_owners = lax.dynamic_slice_in_dim(prompt_row, shard_rank * prompts, prompts, 0)
    my_rows = shard_rank * rows + jnp.arange(rows, dtype=jnp.int32)
    my_lengths = lax.dynamic_slice_in_dim(lengths, shard_rank * rows, rows, 0)
    owned = prompt_row[None, :] == my_rows[:, None]
    is_new = jnp.any(owned, axis=1).astype(jnp.int32)
    pick = jnp.sum(
        jnp.where(owned, jnp.arange(prompt_row.shape[0], dtype=jnp.int32)[None, :], 0), axis=1
    )
    positions = (
        jnp.take(lengths, my_owners)[:, None] + jnp.arange(PLEN, dtype=jnp.int32)[None, :]
    )
    cosine, sine_part = angle_tables(positions, head_size)
    step_ids = jnp.arange(steps, dtype=jnp.int32)
    step_pos = (my_lengths + PLEN * is_new)[None, :] + step_ids[:, None]
    step_pos = jnp.pad(step_pos.reshape(-1), (0, pad - steps * rows))
    step_cos, step_sin = angle_tables(step_pos, head_size)
    step_hidden = jnp.pad(
        decode_hidden.reshape(steps * rows, features), ((0, pad - steps * rows), (0, 0))
    )
    query_units = jnp.transpose(
        queries.reshape(steps, rows, n_t, kpc, unit, head_size), (2, 1, 3, 0, 4, 5)
    ).reshape(n_t, rows, kpc, unit_rows, head_size)

    vmem = pl.BlockSpec(memory_space=pltpu.VMEM)
    smem = pl.BlockSpec(memory_space=pltpu.SMEM)
    hbm = pl.BlockSpec(memory_space=pl.ANY)
    per_unit = (kpc, unit_rows)
    dma = pltpu.SemaphoreType.DMA
    flops = 2 * tokens * features * 2 * cols * n_t
    result = pl.pallas_call(
        functools.partial(kernel, (n_t, n_s, n_seq, kpc, unit, group, steps, rows)),
        out_shape=jax.ShapeDtypeStruct((rows,) + per_unit + (head_size,), bf16),
        in_specs=[hbm, vmem, vmem, hbm, hbm, vmem, vmem, vmem, vmem, vmem]
        + [smem, smem, smem, smem],
        out_specs=vmem,
        scratch_shapes=[
            pltpu.VMEM((tokens + pad, features), bf16),
            pltpu.VMEM((n_t, features, cols), bf16),
            pltpu.VMEM((n_t, features, cols), bf16),
            pltpu.VMEM(kv_cache.shape, bf16),
            pltpu.VMEM((tokens + pad, cols), f32),
            pltpu.VMEM((n_t, prompts, kpc, PLEN, head_size), bf16),
            pltpu.VMEM((n_t, prompts, kpc, PLEN, head_size), bf16),
            pltpu.VMEM((n_s, rows) + per_unit + (head_size,), bf16),
            pltpu.VMEM((n_t, prompts) + per_unit + (head_size,), bf16),
            pltpu.VMEM((n_t, tokens // BLOCK, 8, BLOCK), f32),
            pltpu.VMEM((n_t, pad, LANES), f32),
            pltpu.VMEM((n_t, prompts) + per_unit + (PLEN,), f32),
            pltpu.VMEM((n_t - 1, prompts) + per_unit + (PLEN,), f32),
            pltpu.VMEM((n_t, prompts) + per_unit + (PLEN,), bf16),
            pltpu.VMEM((n_s, prompts) + per_unit + (LANES,), f32),
            pltpu.VMEM((prompts,) + per_unit + (LANES,), f32),
            pltpu.VMEM((n_t, prompts) + per_unit + (head_size,), f32),
            pltpu.VMEM((n_t - 1, prompts) + per_unit + (head_size,), f32),
            pltpu.VMEM((n_s, prompts) + per_unit + (head_size,), bf16),
            pltpu.VMEM((n_t, rows) + per_unit + (head_size,), bf16),
            pltpu.VMEM((n_t - 1, rows) + per_unit + (head_size,), bf16),
            pltpu.VMEM((n_t,) + per_unit + (LANES,), f32),
            pltpu.VMEM((n_t - 1,) + per_unit + (LANES,), f32),
            pltpu.VMEM((n_t, 2, kpc, pad, head_size), f32),
            pltpu.VMEM((n_t - 1, 2, kpc, pad, head_size), f32),
            dma((tokens // BLOCK,)),
            dma((2, kpc, n_t)),
            dma,
            dma((3, 2, n_s - 1)),
            dma((9, 2, n_t - 1)),
        ],
        compiler_params=pltpu.CompilerParams(
            collective_id=0, has_side_effects=True, vmem_limit_bytes=60 * 1024 * 1024
        ),
        cost_estimate=pl.CostEstimate(
            flops=flops, bytes_accessed=30_000_000, transcendentals=1_000_000
        ),
    )(
        prompt_hidden,
        step_hidden,
        norm_gain.reshape(1, features),
        kv_weight,
        kv_cache,
        query_units,
        cosine,
        sine_part,
        step_cos,
        step_sin,
        my_owners,
        my_lengths,
        is_new,
        pick,
    )
    result = result.reshape(rows, kpc, steps, unit, head_size)
    return jnp.transpose(result, (2, 0, 1, 3, 4)).reshape(steps, rows, local_heads * head_size)


def solution(mesh):
    return jax.shard_map(
        per_device,
        mesh=mesh,
        in_specs=(
            P(("group", "seq"), "tensor"),
            P(None, ("group", "seq"), "tensor"),
            P("tensor"),
            P("tensor", None),
            P(("group", "seq"), None, "tensor", None),
            P(None, ("group", "seq"), None),
            P(),
            P(),
        ),
        out_specs=P(None, ("group", "seq"), "tensor"),
        check_vma=False,
    )
```

```python
import functools
import math

import jax
import jax.numpy as jnp
import numpy as np
from jax import lax
from jax.experimental import pallas as pl
from jax.experimental.pallas import tpu as pltpu
from jax.sharding import PartitionSpec as P

D = 12288
PLEN = 768
BLOCK = 256
LANES = 128


epsilon = 1e-05
rope_base = 1000000.0
very_negative = -1e30
f32 = jnp.float32
bf16 = jnp.bfloat16
contract_last = (((1,), (1,)), ((), ()))
contract_inner = (((1,), (0,)), ((), ()))


def angle_tables(head_size):
    halfway = head_size // 2
    frequency = rope_base ** (np.arange(halfway) * (-2.0 / head_size))
    frequency = np.concatenate([frequency, frequency])[None, :]
    angles = np.arange(PLEN)[:, None] * frequency
    signs = np.where(np.arange(head_size) < halfway, -1.0, 1.0)[None, :]
    tables = np.cos(angles), np.sin(angles) * signs, np.concatenate([frequency, signs])
    return [jnp.asarray(table, f32) for table in tables]


def rotated(values, cosine, sine_part):
    return values * cosine + pltpu.roll(values, values.shape[-1] // 2, 1) * sine_part


def kernel(
    sizes,
    prompt_ref,
    step_hidden_ref,
    gain_ref,
    weight_ref,
    cache_ref,
    query_ref,
    cos_ref,
    sin_ref,
    line_ref,
    length_ref,
    prompt_row_ref,
    out_ref,
    xw,
    wk,
    wv,
    cbuf,
    acc,
    kbuf,
    vbuf,
    q1,
    q2,
    sq,
    sqd,
    s_send,
    s_recv,
    w_all,
    lse_all,
    linv,
    o_send,
    o_recv,
    o_all,
    c_send,
    c_recv,
    cl_send,
    cl_recv,
    d_send,
    d_recv,
    cos_at,
    sin_at,
    out_wide,
    x_sem,
    w_sem,
    c_sem,
    shard_sems,
    tensor_sems,
):
    n_t, n_s, n_seq, kpc, unit, group, steps, rows = sizes
    tokens, features = prompt_ref.shape
    prompts = tokens // PLEN
    pad = d_send.shape[3]
    cache_rows = cbuf.shape[2]
    me = lax.axis_index("tensor")
    my_seq = lax.axis_index("seq")
    shard = lax.axis_index("group") * n_seq + my_seq
    scale = 1.0 / math.sqrt(LANES)
    unit_rows = unit * steps

    def chunk(k):
        return lax.rem(me + 1 + k, n_t)

    def head_of(t, j):
        return (t * kpc * unit + j * unit) // group

    def to_tensor(src, dst, which, k):
        return pltpu.make_async_remote_copy(
            src_ref=src,
            dst_ref=dst,
            send_sem=tensor_sems.at[which, 0, k],
            recv_sem=tensor_sems.at[which, 1, k],
            device_id={"tensor": chunk(k)},
            device_id_type=pl.DeviceIdType.MESH,
        )

    def to_shard(src, dst, which, k):
        peer = lax.rem(shard + 1 + k, n_s)
        return pltpu.make_async_remote_copy(
            src_ref=src,
            dst_ref=dst,
            send_sem=shard_sems.at[which, 0, k],
            recv_sem=shard_sems.at[which, 1, k],
            device_id={"group": peer // n_seq, "seq": lax.rem(peer, n_seq)},
            device_id_type=pl.DeviceIdType.MESH,
        )

    def each(count, body):
        def step(k, carry):
            body(k)
            return carry

        lax.fori_loop(0, count, step, 0)

    def gather(maker, ref, mine, which, count):
        each(count, lambda k: maker(ref.at[mine], ref.at[mine], which, k).start())

    def gathered(maker, ref, mine, which, count, total):
        def body(k):
            source = lax.rem(mine - 1 - k + total, total)
            maker(ref.at[mine], ref.at[source], which, k).wait_recv()

        each(count, body)

    def sent(maker, ref, mine, which, count):
        each(count, lambda k: maker(ref.at[mine], ref.at[mine], which, k).wait_send())

    blocks = tokens // BLOCK

    def x_copy(b):
        at = pl.ds(pl.multiple_of(b * BLOCK, BLOCK), BLOCK)
        return pltpu.make_async_copy(prompt_ref.at[at], xw.at[at], x_sem.at[b])

    def w_copy(k, j, value):
        column = pl.multiple_of(head_of(chunk(k), j) * 2 * LANES + value * LANES, LANES)
        dst = (wv if value else wk).at[k, :, pl.ds(j * LANES, LANES)]
        return pltpu.make_async_copy(
            weight_ref.at[:, pl.ds(column, LANES)], dst, w_sem.at[value, j, k]
        )

    c_copy = pltpu.make_async_copy(cache_ref, cbuf, c_sem)
    each(blocks, lambda b: x_copy(b).start())
    for value in range(2):
        for j in range(kpc):
            each(n_t, lambda k: w_copy(k, j, value).start())
    c_copy.start()

    barrier = pltpu.get_barrier_semaphore()

    def greet_tensor(k):
        pl.semaphore_signal(
            barrier, inc=1, device_id={"tensor": chunk(k)}, device_id_type=pl.DeviceIdType.MESH
        )

    def greet_shard(k):
        peer = lax.rem(shard + 1 + k, n_s)
        pl.semaphore_signal(
            barrier,
            inc=1,
            device_id={"group": peer // n_seq, "seq": lax.rem(peer, n_seq)},
            device_id_type=pl.DeviceIdType.MESH,
        )

    each(n_t - 1, greet_tensor)
    each(n_s - 1, greet_shard)
    pl.semaphore_wait(barrier, n_t + n_s - 2)

    owners = [prompt_row_ref[shard * prompts + p] for p in range(prompts)]
    row_lengths = [length_ref[shard * rows + r] for r in range(rows)]
    row_new = [jnp.int32(0) for r in range(rows)]
    row_pick = [jnp.int32(0) for r in range(rows)]
    for i in range(prompt_row_ref.shape[0]):
        row = prompt_row_ref[i]
        for r in range(rows):
            mine = row == shard * rows + r
            row_new[r] = jnp.where(mine, 1, row_new[r])
            row_pick[r] = jnp.where(mine, i, row_pick[r])

    q1[shard] = query_ref[me]
    gather(to_shard, q1, shard, 0, n_s - 1)

    def weigh(b):
        x_copy(b).wait()
        at = pl.ds(pl.multiple_of(b * BLOCK, BLOCK), BLOCK)
        square = jnp.zeros((BLOCK, LANES), f32)
        for c in range(features // LANES):
            lanes = pl.ds(c * LANES, LANES)
            wide = xw[at, lanes].astype(f32)
            square += wide * wide
            xw[at, lanes] = (wide * gain_ref[:, lanes].astype(f32)).astype(bf16)
        total = jnp.sum(square.T, axis=0, keepdims=True)
        sq[me, b] = jnp.broadcast_to(total, (8, BLOCK))

    each(blocks, weigh)
    wide = [step_hidden_ref[step].astype(f32) for step in range(steps)]
    wide.append(jnp.zeros((pad - steps * rows, features), f32))
    wide = jnp.concatenate(wide, axis=0)
    sqd[me] = jnp.broadcast_to(
        jnp.sum(wide * wide, axis=1, keepdims=True), (pad, LANES)
    )
    xw[pl.ds(tokens, pad), :] = (wide * gain_ref[...].astype(f32)).astype(bf16)
    for p in range(prompts):
        start = length_ref[owners[p]].astype(f32) * line_ref[0:1, :]
        start_cos, start_sin = jnp.cos(start), jnp.sin(start)
        signs = line_ref[1:2, :]
        cos_at[p] = cos_ref[...] * start_cos - sin_ref[...] * (start_sin * signs)
        sin_at[p] = sin_ref[...] * start_cos + cos_ref[...] * (start_sin * signs)
    gather(to_tensor, sq, me, 0, n_t - 1)
    gather(to_tensor, sqd, me, 1, n_t - 1)

    def keys(k):
        for j in range(kpc):
            w_copy(k, j, 0).wait()
        acc[...] = jnp.dot(xw[...], wk[k], preferred_element_type=f32)
        for j in range(kpc):
            lanes = pl.ds(j * LANES, LANES)
            for p in range(prompts):
                part = acc[pl.ds(p * PLEN, PLEN), lanes]
                kbuf[k, p, j] = rotated(part, cos_at[p], sin_at[p]).astype(bf16)
            d_send[k, 0, j] = acc[pl.ds(tokens, pad), lanes]

    each(n_t, keys)

    gathered(to_shard, q1, shard, 0, n_s - 1, n_s)
    for p in range(prompts):
        owner = owners[p]
        q2[me, p] = q1[owner // rows, lax.rem(owner, rows)]
    gather(to_tensor, q2, me, 2, n_t - 1)
    gathered(to_tensor, q2, me, 2, n_t - 1, n_t)

    def score(k):
        t = chunk(k)
        for p in range(prompts):
            for j in range(kpc):
                s_send[k, p, j] = lax.dot_general(
                    q2[t, p, j], kbuf[k, p, j], contract_last, preferred_element_type=f32
                )

        @pl.when(k < n_t - 1)
        def _():
            to_tensor(s_send.at[k], s_recv.at[k], 3, k).start()

    each(n_t, score)

    def values(k):
        for j in range(kpc):
            w_copy(k, j, 1).wait()
        acc[...] = jnp.dot(xw[...], wv[k], preferred_element_type=f32)
        for j in range(kpc):
            lanes = pl.ds(j * LANES, LANES)
            for p in range(prompts):
                vbuf[k, p, j] = acc[pl.ds(p * PLEN, PLEN), lanes].astype(bf16)
            d_send[k, 1, j] = acc[pl.ds(tokens, pad), lanes]

        @pl.when(k < n_t - 1)
        def _():
            to_tensor(d_send.at[k], d_recv.at[k], 4, k).start()

    each(n_t, values)

    c_copy.wait()
    position = me * cache_rows + lax.broadcasted_iota(jnp.int32, (unit_rows, cache_rows), 1)
    lane = lax.broadcasted_iota(jnp.int32, (unit_rows, LANES), 1)
    per_row = LANES // rows

    def resident(k):
        t = chunk(k)
        for j in range(kpc):
            g = head_of(t, j)
            packed = jnp.zeros((unit_rows, LANES), f32)
            for r in range(rows):
                found = lax.dot_general(
                    query_ref[t, r, j],
                    cbuf[r, g, :, pl.ds(0, LANES)],
                    contract_last,
                    preferred_element_type=f32,
                )
                mask = position < row_lengths[r]
                found = jnp.where(mask, found * scale, very_negative)
                top = jnp.max(found, axis=1, keepdims=True)
                weights = jnp.where(mask, jnp.exp(found - top), 0.0)
                total = jnp.sum(weights, axis=1, keepdims=True)
                some = total > 0.0
                total = jnp.where(some, total, 1.0)
                mixed = lax.dot_general(
                    weights.astype(bf16),
                    cbuf[r, g, :, pl.ds(LANES, LANES)],
                    contract_inner,
                    preferred_element_type=f32,
                )
                c_send[k, r, j] = (mixed / total).astype(bf16)
                log = jnp.where(some, top + jnp.log(total), very_negative)
                packed = jnp.where(lane // per_row == r, log, packed)
            cl_send[k, j] = packed

        @pl.when(k < n_t - 1)
        def _():
            to_tensor(c_send.at[k], c_recv.at[k], 5, k).start()
            to_tensor(cl_send.at[k], cl_recv.at[k], 6, k).start()

    each(n_t, resident)

    gathered(to_tensor, sq, me, 0, n_t - 1, n_t)
    gathered(to_tensor, sqd, me, 1, n_t - 1, n_t)
    each(n_t - 1, lambda k: to_tensor(s_send.at[k], s_recv.at[k], 3, k).wait_recv())
    per_prompt = PLEN // BLOCK
    for p in range(prompts):
        parts = []
        for b in range(per_prompt):
            total = sq[0, p * per_prompt + b]
            for t in range(1, n_t):
                total += sq[t, p * per_prompt + b]
            parts.append(lax.rsqrt(total[0:1] / D + epsilon))
        factor = jnp.concatenate(parts, axis=1)
        for j in range(kpc):
            total = s_send[n_t - 1, p, j]
            for k in range(n_t - 1):
                total += s_recv[k, p, j]
            total = total * (factor * scale)
            top = jnp.max(total, axis=1, keepdims=True)
            weights = jnp.exp(total - top)
            whole = jnp.sum(weights, axis=1, keepdims=True)
            w_all[me, p, j] = (weights * factor).astype(bf16)
            lse_all[shard, p, j] = jnp.broadcast_to(top + jnp.log(whole), (unit_rows, LANES))
            linv[p, j] = jnp.broadcast_to(1.0 / whole, (unit_rows, LANES))
    gather(to_tensor, w_all, me, 7, n_t - 1)
    gather(to_shard, lse_all, shard, 1, n_s - 1)

    def mix(k):
        t = chunk(k)

        @pl.when(k < n_t - 1)
        def _():
            to_tensor(w_all.at[me], w_all.at[t], 7, n_t - 2 - k).wait_recv()

        for p in range(prompts):
            for j in range(kpc):
                o_send[k, p, j] = lax.dot_general(
                    w_all[t, p, j], vbuf[k, p, j], contract_inner, preferred_element_type=f32
                )

        @pl.when(k < n_t - 1)
        def _():
            to_tensor(o_send.at[k], o_recv.at[k], 8, k).start()

    each(n_t, mix)
    each(n_t - 1, lambda k: to_tensor(o_send.at[k], o_recv.at[k], 8, k).wait_recv())
    for p in range(prompts):
        for j in range(kpc):
            total = o_send[n_t - 1, p, j]
            for k in range(n_t - 1):
                total += o_recv[k, p, j]
            o_all[shard, p, j] = (total * linv[p, j]).astype(bf16)
    gather(to_shard, o_all, shard, 2, n_s - 1)

    each(n_t - 1, lambda k: to_tensor(d_send.at[k], d_recv.at[k], 4, k).wait_recv())
    each(n_t - 1, lambda k: to_tensor(c_send.at[k], c_recv.at[k], 5, k).wait_recv())
    each(n_t - 1, lambda k: to_tensor(cl_send.at[k], cl_recv.at[k], 6, k).wait_recv())
    total = sqd[0]
    for t in range(1, n_t):
        total += sqd[t]
    factor = lax.rsqrt(total / D + epsilon)
    own_row = lax.broadcasted_iota(jnp.int32, (unit_rows, pad), 0)
    column = lax.broadcasted_iota(jnp.int32, (unit_rows, pad), 1)
    causal = (column // rows <= own_row // unit) & (column < steps * rows)
    spot = lax.broadcasted_iota(jnp.int32, (pad, LANES), 0)
    place = jnp.zeros((pad, LANES), jnp.int32)
    for r in range(rows):
        start = row_lengths[r] + PLEN * row_new[r]
        place = jnp.where(lax.rem(spot, rows) == r, start + spot // rows, place)
    angles = place.astype(f32) * line_ref[0:1, :]
    step_cos, step_sin = jnp.cos(angles), jnp.sin(angles) * line_ref[1:2, :]
    states = {}
    for j in range(kpc):
        terms = []
        for value in range(2):
            total = d_send[n_t - 1, value, j]
            for k in range(n_t - 1):
                total += d_recv[k, value, j]
            terms.append(total * factor)
        key = rotated(terms[0], step_cos, step_sin).astype(bf16)
        value = terms[1].astype(bf16)
        for r in range(rows):
            found = lax.dot_general(
                query_ref[me, r, j], key, contract_last, preferred_element_type=f32
            )
            mask = causal & (lax.rem(column, rows) == r)
            found = jnp.where(mask, found * scale, very_negative)
            top = jnp.max(found, axis=1, keepdims=True)
            logs = [cl_send[n_t - 1, j][:, r * per_row : r * per_row + 1]]
            outs = [c_send[n_t - 1, r, j]]
            for k in range(n_t - 1):
                logs.append(cl_recv[k, j][:, r * per_row : r * per_row + 1])
                outs.append(c_recv[k, r, j])
            for log in logs:
                top = jnp.maximum(top, log)
            weights = jnp.where(mask, jnp.exp(found - top), 0.0)
            whole = jnp.sum(weights, axis=1, keepdims=True)
            mixed = lax.dot_general(
                weights.astype(bf16), value, contract_inner, preferred_element_type=f32
            )
            for log, out in zip(logs, outs):
                share = jnp.exp(log - top)
                whole += share
                mixed += share * out.astype(f32)
            states[j, r] = (top, whole, mixed)

    gathered(to_shard, lse_all, shard, 1, n_s - 1, n_s)
    gathered(to_shard, o_all, shard, 2, n_s - 1, n_s)
    for j in range(kpc):
        for r in range(rows):
            top, whole, mixed = states[j, r]
            pick = row_pick[r]
            source, p = pick // prompts, lax.rem(pick, prompts)
            log = lse_all[source, p, j]
            log = jnp.where(row_new[r] > 0, log, very_negative)
            out = o_all[source, p, j].astype(f32)
            last = jnp.maximum(top, log)
            left, right = jnp.exp(top - last), jnp.exp(log - last)
            out = (mixed * left + out * right) / (whole * left + right)
            for step in range(steps):
                for h in range(unit):
                    lanes = pl.ds((j * unit + h) * LANES, LANES)
                    at = step * unit + h
                    out_wide[step, r : r + 1, lanes] = out[at : at + 1, :]
    out_ref[...] = out_wide[...].astype(bf16)

    sent(to_shard, q1, shard, 0, n_s - 1)
    sent(to_shard, lse_all, shard, 1, n_s - 1)
    sent(to_shard, o_all, shard, 2, n_s - 1)
    sent(to_tensor, sq, me, 0, n_t - 1)
    sent(to_tensor, sqd, me, 1, n_t - 1)
    sent(to_tensor, q2, me, 2, n_t - 1)
    sent(to_tensor, w_all, me, 7, n_t - 1)
    for which, src, dst in (
        (3, s_send, s_recv),
        (4, d_send, d_recv),
        (5, c_send, c_recv),
        (6, cl_send, cl_recv),
        (8, o_send, o_recv),
    ):
        each(n_t - 1, lambda k: to_tensor(src.at[k], dst.at[k], which, k).wait_send())


def per_device(
    prompt_hidden, decode_hidden, norm_gain, kv_weight, kv_cache, queries, lengths, prompt_row
):
    shards = ("group", "seq")
    n_t = lax.axis_size("tensor")
    n_s = lax.axis_size(shards)
    n_seq = lax.axis_size("seq")
    tokens, features = prompt_hidden.shape
    steps, rows, query_width = queries.shape
    kv_heads, cache_rows = kv_cache.shape[1:3]
    head_size = kv_cache.shape[3] // 2
    query_heads = query_width // head_size
    group = query_heads // kv_heads
    local_heads = query_heads // n_t
    unit = min(local_heads, group)
    kpc = local_heads // unit
    prompts = tokens // PLEN
    unit_rows = unit * steps
    pad = -(-steps * rows // 16) * 16
    cols = kpc * head_size

    cosine, sine_part, line = angle_tables(head_size)
    query_units = jnp.transpose(
        queries.reshape(steps, rows, n_t, kpc, unit, head_size), (2, 1, 3, 0, 4, 5)
    ).reshape(n_t, rows, kpc, unit_rows, head_size)

    vmem = pl.BlockSpec(memory_space=pltpu.VMEM)
    smem = pl.BlockSpec(memory_space=pltpu.SMEM)
    hbm = pl.BlockSpec(memory_space=pl.ANY)
    per_unit = (kpc, unit_rows)
    dma = pltpu.SemaphoreType.DMA
    flops = 2 * tokens * features * 2 * cols * n_t
    return pl.pallas_call(
        functools.partial(kernel, (n_t, n_s, n_seq, kpc, unit, group, steps, rows)),
        out_shape=jax.ShapeDtypeStruct((steps, rows, local_heads * head_size), bf16),
        in_specs=[hbm, vmem, vmem, hbm, hbm, vmem, vmem, vmem, vmem]
        + [smem, smem],
        out_specs=vmem,
        scratch_shapes=[
            pltpu.VMEM((tokens + pad, features), bf16),
            pltpu.VMEM((n_t, features, cols), bf16),
            pltpu.VMEM((n_t, features, cols), bf16),
            pltpu.VMEM(kv_cache.shape, bf16),
            pltpu.VMEM((tokens + pad, cols), f32),
            pltpu.VMEM((n_t, prompts, kpc, PLEN, head_size), bf16),
            pltpu.VMEM((n_t, prompts, kpc, PLEN, head_size), bf16),
            pltpu.VMEM((n_s, rows) + per_unit + (head_size,), bf16),
            pltpu.VMEM((n_t, prompts) + per_unit + (head_size,), bf16),
            pltpu.VMEM((n_t, tokens // BLOCK, 8, BLOCK), f32),
            pltpu.VMEM((n_t, pad, LANES), f32),
            pltpu.VMEM((n_t, prompts) + per_unit + (PLEN,), f32),
            pltpu.VMEM((n_t - 1, prompts) + per_unit + (PLEN,), f32),
            pltpu.VMEM((n_t, prompts) + per_unit + (PLEN,), bf16),
            pltpu.VMEM((n_s, prompts) + per_unit + (LANES,), f32),
            pltpu.VMEM((prompts,) + per_unit + (LANES,), f32),
            pltpu.VMEM((n_t, prompts) + per_unit + (head_size,), f32),
            pltpu.VMEM((n_t - 1, prompts) + per_unit + (head_size,), f32),
            pltpu.VMEM((n_s, prompts) + per_unit + (head_size,), bf16),
            pltpu.VMEM((n_t, rows) + per_unit + (head_size,), bf16),
            pltpu.VMEM((n_t - 1, rows) + per_unit + (head_size,), bf16),
            pltpu.VMEM((n_t,) + per_unit + (LANES,), f32),
            pltpu.VMEM((n_t - 1,) + per_unit + (LANES,), f32),
            pltpu.VMEM((n_t, 2, kpc, pad, head_size), f32),
            pltpu.VMEM((n_t - 1, 2, kpc, pad, head_size), f32),
            pltpu.VMEM((prompts, PLEN, head_size), f32),
            pltpu.VMEM((prompts, PLEN, head_size), f32),
            pltpu.VMEM((steps, rows, local_heads * head_size), f32),
            dma((tokens // BLOCK,)),
            dma((2, kpc, n_t)),
            dma,
            dma((3, 2, n_s - 1)),
            dma((9, 2, n_t - 1)),
        ],
        compiler_params=pltpu.CompilerParams(
            collective_id=0, has_side_effects=True, vmem_limit_bytes=60 * 1024 * 1024
        ),
        cost_estimate=pl.CostEstimate(
            flops=flops, bytes_accessed=30_000_000, transcendentals=1_000_000
        ),
    )(
        prompt_hidden,
        decode_hidden,
        norm_gain.reshape(1, features),
        kv_weight,
        kv_cache,
        query_units,
        cosine,
        sine_part,
        line,
        lengths,
        prompt_row,
    )


def solution(mesh):
    return jax.shard_map(
        per_device,
        mesh=mesh,
        in_specs=(
            P(("group", "seq"), "tensor"),
            P(None, ("group", "seq"), "tensor"),
            P("tensor"),
            P("tensor", None),
            P(("group", "seq"), None, "tensor", None),
            P(None, ("group", "seq"), None),
            P(),
            P(),
        ),
        out_specs=P(None, ("group", "seq"), "tensor"),
        check_vma=False,
    )
```

```python
import functools
import math

import jax
import jax.numpy as jnp
import numpy as np
from jax import lax
from jax.experimental import pallas as pl
from jax.experimental.pallas import tpu as pltpu
from jax.sharding import PartitionSpec as P

D = 12288
PLEN = 768
BLOCK = 256
LANES = 128


epsilon = 1e-05
rope_base = 1000000.0
very_negative = -1e30
f32 = jnp.float32
bf16 = jnp.bfloat16
contract_last = (((1,), (1,)), ((), ()))
contract_inner = (((1,), (0,)), ((), ()))


def angle_tables(head_size):
    halfway = head_size // 2
    frequency = rope_base ** (np.arange(halfway) * (-2.0 / head_size))
    frequency = np.concatenate([frequency, frequency])[None, :]
    angles = np.arange(PLEN)[:, None] * frequency
    signs = np.where(np.arange(head_size) < halfway, -1.0, 1.0)[None, :]
    tables = np.cos(angles), np.sin(angles) * signs, np.concatenate([frequency, signs])
    return [jnp.asarray(table, f32) for table in tables]


def rotated(values, cosine, sine_part):
    return values * cosine + pltpu.roll(values, values.shape[-1] // 2, 1) * sine_part


def kernel(
    sizes,
    prompt_ref,
    step_hidden_ref,
    gain_ref,
    weight_ref,
    cache_ref,
    query_ref,
    cos_ref,
    sin_ref,
    line_ref,
    length_ref,
    prompt_row_ref,
    out_ref,
    xw,
    wk,
    wv,
    cbuf,
    acc,
    kbuf,
    vbuf,
    q1,
    q2,
    sq,
    sqd,
    s_send,
    s_recv,
    w_all,
    lse_all,
    linv,
    o_send,
    o_recv,
    o_all,
    c_send,
    c_recv,
    cl_send,
    cl_recv,
    d_send,
    d_recv,
    cos_at,
    sin_at,
    out_wide,
    s_own,
    x_sem,
    w_sem,
    c_sem,
    shard_sems,
    tensor_sems,
):
    n_t, n_s, n_seq, kpc, unit, group, steps, rows = sizes
    tokens, features = prompt_ref.shape
    prompts = tokens // PLEN
    pad = d_send.shape[3]
    cache_rows = cbuf.shape[2]
    me = lax.axis_index("tensor")
    my_seq = lax.axis_index("seq")
    shard = lax.axis_index("group") * n_seq + my_seq
    scale = 1.0 / math.sqrt(LANES)
    unit_rows = unit * steps

    def chunk(k):
        return lax.rem(me + 1 + k, n_t)

    def head_of(t, j):
        return (t * kpc * unit + j * unit) // group

    def to_tensor(src, dst, which, k):
        return pltpu.make_async_remote_copy(
            src_ref=src,
            dst_ref=dst,
            send_sem=tensor_sems.at[which, 0, k],
            recv_sem=tensor_sems.at[which, 1, k],
            device_id={"tensor": chunk(k)},
            device_id_type=pl.DeviceIdType.MESH,
        )

    def to_shard(src, dst, which, k):
        peer = lax.rem(shard + 1 + k, n_s)
        return pltpu.make_async_remote_copy(
            src_ref=src,
            dst_ref=dst,
            send_sem=shard_sems.at[which, 0, k],
            recv_sem=shard_sems.at[which, 1, k],
            device_id={"group": peer // n_seq, "seq": lax.rem(peer, n_seq)},
            device_id_type=pl.DeviceIdType.MESH,
        )

    def each(count, body):
        def step(k, carry):
            body(k)
            return carry

        lax.fori_loop(0, count, step, 0)

    def gather(maker, ref, mine, which, count):
        each(count, lambda k: maker(ref.at[mine], ref.at[mine], which, k).start())

    def gathered(maker, ref, mine, which, count, total):
        def body(k):
            source = lax.rem(mine - 1 - k + total, total)
            maker(ref.at[mine], ref.at[source], which, k).wait_recv()

        each(count, body)

    def sent(maker, ref, mine, which, count):
        each(count, lambda k: maker(ref.at[mine], ref.at[mine], which, k).wait_send())

    blocks = tokens // BLOCK

    def x_copy(b):
        at = pl.ds(pl.multiple_of(b * BLOCK, BLOCK), BLOCK)
        return pltpu.make_async_copy(prompt_ref.at[at], xw.at[at], x_sem.at[b])

    def w_copy(k, j, value):
        column = pl.multiple_of(head_of(chunk(k), j) * 2 * LANES + value * LANES, LANES)
        dst = (wv if value else wk).at[k, :, pl.ds(j * LANES, LANES)]
        return pltpu.make_async_copy(
            weight_ref.at[:, pl.ds(column, LANES)], dst, w_sem.at[value, j, k]
        )

    c_copy = pltpu.make_async_copy(cache_ref, cbuf, c_sem)
    c_copy.start()
    each(blocks, lambda b: x_copy(b).start())
    for value in range(2):
        for j in range(kpc):
            each(n_t, lambda k: w_copy(k, j, value).start())

    barrier = pltpu.get_barrier_semaphore()

    def greet_tensor(k):
        pl.semaphore_signal(
            barrier, inc=1, device_id={"tensor": chunk(k)}, device_id_type=pl.DeviceIdType.MESH
        )

    def greet_shard(k):
        peer = lax.rem(shard + 1 + k, n_s)
        pl.semaphore_signal(
            barrier,
            inc=1,
            device_id={"group": peer // n_seq, "seq": lax.rem(peer, n_seq)},
            device_id_type=pl.DeviceIdType.MESH,
        )

    each(n_t - 1, greet_tensor)
    each(n_s - 1, greet_shard)
    pl.semaphore_wait(barrier, n_t + n_s - 2)

    owners = [prompt_row_ref[shard * prompts + p] for p in range(prompts)]
    row_lengths = [length_ref[shard * rows + r] for r in range(rows)]
    row_new = [jnp.int32(0) for r in range(rows)]
    row_pick = [jnp.int32(0) for r in range(rows)]
    for i in range(prompt_row_ref.shape[0]):
        row = prompt_row_ref[i]
        for r in range(rows):
            mine = row == shard * rows + r
            row_new[r] = jnp.where(mine, 1, row_new[r])
            row_pick[r] = jnp.where(mine, i, row_pick[r])

    q1[shard] = query_ref[me]
    gather(to_shard, q1, shard, 0, n_s - 1)

    c_copy.wait()
    position = me * cache_rows + lax.broadcasted_iota(jnp.int32, (unit_rows, cache_rows), 1)
    lane = lax.broadcasted_iota(jnp.int32, (unit_rows, LANES), 1)
    per_row = LANES // rows

    def resident(k):
        t = chunk(k)
        for j in range(kpc):
            g = head_of(t, j)
            packed = jnp.zeros((unit_rows, LANES), f32)
            for r in range(rows):
                found = lax.dot_general(
                    query_ref[t, r, j],
                    cbuf[r, g, :, pl.ds(0, LANES)],
                    contract_last,
                    preferred_element_type=f32,
                )
                mask = position < row_lengths[r]
                found = jnp.where(mask, found * scale, very_negative)
                top = jnp.max(found, axis=1, keepdims=True)
                weights = jnp.where(mask, jnp.exp(found - top), 0.0)
                total = jnp.sum(weights, axis=1, keepdims=True)
                some = total > 0.0
                total = jnp.where(some, total, 1.0)
                mixed = lax.dot_general(
                    weights.astype(bf16),
                    cbuf[r, g, :, pl.ds(LANES, LANES)],
                    contract_inner,
                    preferred_element_type=f32,
                )
                c_send[k, r, j] = (mixed / total).astype(bf16)
                log = jnp.where(some, top + jnp.log(total), very_negative)
                packed = jnp.where(lane // per_row == r, log, packed)
            cl_send[k, j] = packed

        @pl.when(k < n_t - 1)
        def _():
            to_tensor(c_send.at[k], c_recv.at[k], 5, k).start()
            to_tensor(cl_send.at[k], cl_recv.at[k], 6, k).start()

    each(n_t, resident)


    gains = [gain_ref[pl.ds(c * LANES, LANES)][None, :] for c in range(features // LANES)]

    def weigh(b):
        x_copy(b).wait()
        at = pl.ds(pl.multiple_of(b * BLOCK, BLOCK), BLOCK)
        square = jnp.zeros((BLOCK, LANES), f32)
        for c in range(features // LANES):
            lanes = pl.ds(c * LANES, LANES)
            part = xw[at, lanes]
            wide = part.astype(f32)
            square += wide * wide
            xw[at, lanes] = part * gains[c]
        total = jnp.sum(square.T, axis=0, keepdims=True)
        sq[me, b] = jnp.broadcast_to(total, (8, BLOCK))

    each(blocks, weigh)
    wide = [step_hidden_ref[step].astype(f32) for step in range(steps)]
    wide.append(jnp.zeros((pad - steps * rows, features), f32))
    wide = jnp.concatenate(wide, axis=0)
    sqd[me] = jnp.broadcast_to(
        jnp.sum(wide * wide, axis=1, keepdims=True), (pad, LANES)
    )
    xw[pl.ds(tokens, pad), :] = (wide * gain_ref[...].astype(f32)[None, :]).astype(bf16)
    for p in range(prompts):
        start = length_ref[owners[p]].astype(f32) * line_ref[0:1, :]
        start_cos, start_sin = jnp.cos(start), jnp.sin(start)
        signs = line_ref[1:2, :]
        cos_at[p] = cos_ref[...] * start_cos - sin_ref[...] * (start_sin * signs)
        sin_at[p] = sin_ref[...] * start_cos + cos_ref[...] * (start_sin * signs)
    gather(to_tensor, sq, me, 0, n_t - 1)
    gather(to_tensor, sqd, me, 1, n_t - 1)

    def keys(k):
        for j in range(kpc):
            w_copy(k, j, 0).wait()
        acc[...] = jnp.dot(xw[...], wk[k], preferred_element_type=f32)
        for j in range(kpc):
            lanes = pl.ds(j * LANES, LANES)
            for p in range(prompts):
                part = acc[pl.ds(p * PLEN, PLEN), lanes]
                kbuf[k, p, j] = rotated(part, cos_at[p], sin_at[p]).astype(bf16)
            d_send[k, 0, j] = acc[pl.ds(tokens, pad), lanes]

    early = n_t // 2
    each(early, keys)

    gathered(to_shard, q1, shard, 0, n_s - 1, n_s)
    for p in range(prompts):
        owner = owners[p]
        q2[me, p] = q1[owner // rows, lax.rem(owner, rows)]
    gather(to_tensor, q2, me, 2, n_t - 1)
    gathered(to_tensor, q2, me, 2, n_t - 1, n_t)

    def score(k):
        t = chunk(k)
        for p in range(prompts):
            for j in range(kpc):
                part = lax.dot_general(
                    q2[t, p, j], kbuf[k, p, j], contract_last, preferred_element_type=f32
                )
                s_own[p, j] = part
                s_send[k, p, j] = part.astype(bf16)

        @pl.when(k < n_t - 1)
        def _():
            to_tensor(s_send.at[k], s_recv.at[k], 3, k).start()

    each(early, score)

    def late(k):
        keys(k + early)
        score(k + early)

    each(n_t - early, late)

    def values(k):
        for j in range(kpc):
            w_copy(k, j, 1).wait()
        acc[...] = jnp.dot(xw[...], wv[k], preferred_element_type=f32)
        for j in range(kpc):
            lanes = pl.ds(j * LANES, LANES)
            for p in range(prompts):
                vbuf[k, p, j] = acc[pl.ds(p * PLEN, PLEN), lanes].astype(bf16)
            d_send[k, 1, j] = acc[pl.ds(tokens, pad), lanes]

        @pl.when(k < n_t - 1)
        def _():
            to_tensor(d_send.at[k], d_recv.at[k], 4, k).start()

    each(n_t, values)

    gathered(to_tensor, sq, me, 0, n_t - 1, n_t)
    gathered(to_tensor, sqd, me, 1, n_t - 1, n_t)
    each(n_t - 1, lambda k: to_tensor(s_send.at[k], s_recv.at[k], 3, k).wait_recv())
    per_prompt = PLEN // BLOCK
    for p in range(prompts):
        parts = []
        for b in range(per_prompt):
            total = sq[0, p * per_prompt + b]
            for t in range(1, n_t):
                total += sq[t, p * per_prompt + b]
            parts.append(lax.rsqrt(total[0:1] / D + epsilon))
        factor = jnp.concatenate(parts, axis=1)
        for j in range(kpc):
            total = s_own[p, j]
            for k in range(n_t - 1):
                total += s_recv[k, p, j].astype(f32)
            total = total * (factor * scale)
            top = jnp.max(total, axis=1, keepdims=True)
            weights = jnp.exp(total - top)
            whole = jnp.sum(weights, axis=1, keepdims=True)
            w_all[me, p, j] = (weights * factor).astype(bf16)
            lse_all[shard, p, j] = jnp.broadcast_to(top + jnp.log(whole), (unit_rows, LANES))
            linv[p, j] = jnp.broadcast_to(1.0 / whole, (unit_rows, LANES))
    gather(to_tensor, w_all, me, 7, n_t - 1)
    gather(to_shard, lse_all, shard, 1, n_s - 1)

    def mix(k):
        t = chunk(k)

        @pl.when(k < n_t - 1)
        def _():
            to_tensor(w_all.at[me], w_all.at[t], 7, n_t - 2 - k).wait_recv()

        for p in range(prompts):
            for j in range(kpc):
                o_send[k, p, j] = lax.dot_general(
                    w_all[t, p, j], vbuf[k, p, j], contract_inner, preferred_element_type=f32
                )

        @pl.when(k < n_t - 1)
        def _():
            to_tensor(o_send.at[k], o_recv.at[k], 8, k).start()

    each(n_t, mix)
    each(n_t - 1, lambda k: to_tensor(o_send.at[k], o_recv.at[k], 8, k).wait_recv())
    for p in range(prompts):
        for j in range(kpc):
            total = o_send[n_t - 1, p, j]
            for k in range(n_t - 1):
                total += o_recv[k, p, j]
            o_all[shard, p, j] = (total * linv[p, j]).astype(bf16)
    gather(to_shard, o_all, shard, 2, n_s - 1)

    each(n_t - 1, lambda k: to_tensor(d_send.at[k], d_recv.at[k], 4, k).wait_recv())
    each(n_t - 1, lambda k: to_tensor(c_send.at[k], c_recv.at[k], 5, k).wait_recv())
    each(n_t - 1, lambda k: to_tensor(cl_send.at[k], cl_recv.at[k], 6, k).wait_recv())
    total = sqd[0]
    for t in range(1, n_t):
        total += sqd[t]
    factor = lax.rsqrt(total / D + epsilon)
    own_row = lax.broadcasted_iota(jnp.int32, (unit_rows, pad), 0)
    column = lax.broadcasted_iota(jnp.int32, (unit_rows, pad), 1)
    causal = (column // rows <= own_row // unit) & (column < steps * rows)
    spot = lax.broadcasted_iota(jnp.int32, (pad, LANES), 0)
    place = jnp.zeros((pad, LANES), jnp.int32)
    for r in range(rows):
        start = row_lengths[r] + PLEN * row_new[r]
        place = jnp.where(lax.rem(spot, rows) == r, start + spot // rows, place)
    angles = place.astype(f32) * line_ref[0:1, :]
    step_cos, step_sin = jnp.cos(angles), jnp.sin(angles) * line_ref[1:2, :]
    states = {}
    for j in range(kpc):
        terms = []
        for value in range(2):
            total = d_send[n_t - 1, value, j]
            for k in range(n_t - 1):
                total += d_recv[k, value, j]
            terms.append(total * factor)
        key = rotated(terms[0], step_cos, step_sin).astype(bf16)
        value = terms[1].astype(bf16)
        for r in range(rows):
            found = lax.dot_general(
                query_ref[me, r, j], key, contract_last, preferred_element_type=f32
            )
            mask = causal & (lax.rem(column, rows) == r)
            found = jnp.where(mask, found * scale, very_negative)
            top = jnp.max(found, axis=1, keepdims=True)
            logs = [cl_send[n_t - 1, j][:, r * per_row : r * per_row + 1]]
            outs = [c_send[n_t - 1, r, j]]
            for k in range(n_t - 1):
                logs.append(cl_recv[k, j][:, r * per_row : r * per_row + 1])
                outs.append(c_recv[k, r, j])
            for log in logs:
                top = jnp.maximum(top, log)
            weights = jnp.where(mask, jnp.exp(found - top), 0.0)
            whole = jnp.sum(weights, axis=1, keepdims=True)
            mixed = lax.dot_general(
                weights.astype(bf16), value, contract_inner, preferred_element_type=f32
            )
            for log, out in zip(logs, outs):
                share = jnp.exp(log - top)
                whole += share
                mixed += share * out.astype(f32)
            states[j, r] = (top, whole, mixed)

    gathered(to_shard, lse_all, shard, 1, n_s - 1, n_s)
    gathered(to_shard, o_all, shard, 2, n_s - 1, n_s)
    for j in range(kpc):
        for r in range(rows):
            top, whole, mixed = states[j, r]
            pick = row_pick[r]
            source, p = pick // prompts, lax.rem(pick, prompts)
            log = lse_all[source, p, j]
            log = jnp.where(row_new[r] > 0, log, very_negative)
            out = o_all[source, p, j].astype(f32)
            last = jnp.maximum(top, log)
            left, right = jnp.exp(top - last), jnp.exp(log - last)
            out = (mixed * left + out * right) / (whole * left + right)
            for step in range(steps):
                for h in range(unit):
                    lanes = pl.ds((j * unit + h) * LANES, LANES)
                    at = step * unit + h
                    out_wide[step, r : r + 1, lanes] = out[at : at + 1, :]
    out_ref[...] = out_wide[...].astype(bf16)

    sent(to_shard, q1, shard, 0, n_s - 1)
    sent(to_shard, lse_all, shard, 1, n_s - 1)
    sent(to_shard, o_all, shard, 2, n_s - 1)
    sent(to_tensor, sq, me, 0, n_t - 1)
    sent(to_tensor, sqd, me, 1, n_t - 1)
    sent(to_tensor, q2, me, 2, n_t - 1)
    sent(to_tensor, w_all, me, 7, n_t - 1)
    for which, src, dst in (
        (3, s_send, s_recv),
        (4, d_send, d_recv),
        (5, c_send, c_recv),
        (6, cl_send, cl_recv),
        (8, o_send, o_recv),
    ):
        each(n_t - 1, lambda k: to_tensor(src.at[k], dst.at[k], which, k).wait_send())


def per_device(
    prompt_hidden, decode_hidden, norm_gain, kv_weight, kv_cache, queries, lengths, prompt_row
):
    shards = ("group", "seq")
    n_t = lax.axis_size("tensor")
    n_s = lax.axis_size(shards)
    n_seq = lax.axis_size("seq")
    tokens, features = prompt_hidden.shape
    steps, rows, query_width = queries.shape
    kv_heads, cache_rows = kv_cache.shape[1:3]
    head_size = kv_cache.shape[3] // 2
    query_heads = query_width // head_size
    group = query_heads // kv_heads
    local_heads = query_heads // n_t
    unit = min(local_heads, group)
    kpc = local_heads // unit
    prompts = tokens // PLEN
    unit_rows = unit * steps
    pad = -(-steps * rows // 16) * 16
    cols = kpc * head_size

    cosine, sine_part, line = angle_tables(head_size)
    query_units = jnp.transpose(
        queries.reshape(steps, rows, n_t, kpc, unit, head_size), (2, 1, 3, 0, 4, 5)
    ).reshape(n_t, rows, kpc, unit_rows, head_size)

    vmem = pl.BlockSpec(memory_space=pltpu.VMEM)
    smem = pl.BlockSpec(memory_space=pltpu.SMEM)
    hbm = pl.BlockSpec(memory_space=pl.ANY)
    per_unit = (kpc, unit_rows)
    dma = pltpu.SemaphoreType.DMA
    flops = 2 * tokens * features * 2 * cols * n_t
    return pl.pallas_call(
        functools.partial(kernel, (n_t, n_s, n_seq, kpc, unit, group, steps, rows)),
        out_shape=jax.ShapeDtypeStruct((steps, rows, local_heads * head_size), bf16),
        in_specs=[hbm, vmem, vmem, hbm, hbm, vmem, vmem, vmem, vmem]
        + [smem, smem],
        out_specs=vmem,
        scratch_shapes=[
            pltpu.VMEM((tokens + pad, features), bf16),
            pltpu.VMEM((n_t, features, cols), bf16),
            pltpu.VMEM((n_t, features, cols), bf16),
            pltpu.VMEM(kv_cache.shape, bf16),
            pltpu.VMEM((tokens + pad, cols), f32),
            pltpu.VMEM((n_t, prompts, kpc, PLEN, head_size), bf16),
            pltpu.VMEM((n_t, prompts, kpc, PLEN, head_size), bf16),
            pltpu.VMEM((n_s, rows) + per_unit + (head_size,), bf16),
            pltpu.VMEM((n_t, prompts) + per_unit + (head_size,), bf16),
            pltpu.VMEM((n_t, tokens // BLOCK, 8, BLOCK), f32),
            pltpu.VMEM((n_t, pad, LANES), f32),
            pltpu.VMEM((n_t, prompts) + per_unit + (PLEN,), bf16),
            pltpu.VMEM((n_t - 1, prompts) + per_unit + (PLEN,), bf16),
            pltpu.VMEM((n_t, prompts) + per_unit + (PLEN,), bf16),
            pltpu.VMEM((n_s, prompts) + per_unit + (LANES,), f32),
            pltpu.VMEM((prompts,) + per_unit + (LANES,), f32),
            pltpu.VMEM((n_t, prompts) + per_unit + (head_size,), f32),
            pltpu.VMEM((n_t - 1, prompts) + per_unit + (head_size,), f32),
            pltpu.VMEM((n_s, prompts) + per_unit + (head_size,), bf16),
            pltpu.VMEM((n_t, rows) + per_unit + (head_size,), bf16),
            pltpu.VMEM((n_t - 1, rows) + per_unit + (head_size,), bf16),
            pltpu.VMEM((n_t,) + per_unit + (LANES,), f32),
            pltpu.VMEM((n_t - 1,) + per_unit + (LANES,), f32),
            pltpu.VMEM((n_t, 2, kpc, pad, head_size), f32),
            pltpu.VMEM((n_t - 1, 2, kpc, pad, head_size), f32),
            pltpu.VMEM((prompts, PLEN, head_size), f32),
            pltpu.VMEM((prompts, PLEN, head_size), f32),
            pltpu.VMEM((steps, rows, local_heads * head_size), f32),
            pltpu.VMEM((prompts,) + per_unit + (PLEN,), f32),
            dma((tokens // BLOCK,)),
            dma((2, kpc, n_t)),
            dma,
            dma((3, 2, n_s - 1)),
            dma((9, 2, n_t - 1)),
        ],
        compiler_params=pltpu.CompilerParams(
            collective_id=0, has_side_effects=True, vmem_limit_bytes=60 * 1024 * 1024
        ),
        cost_estimate=pl.CostEstimate(
            flops=flops, bytes_accessed=30_000_000, transcendentals=1_000_000
        ),
    )(
        prompt_hidden,
        decode_hidden,
        norm_gain,
        kv_weight,
        kv_cache,
        query_units,
        cosine,
        sine_part,
        line,
        lengths,
        prompt_row,
    )


def solution(mesh):
    return jax.shard_map(
        per_device,
        mesh=mesh,
        in_specs=(
            P(("group", "seq"), "tensor"),
            P(None, ("group", "seq"), "tensor"),
            P("tensor"),
            P("tensor", None),
            P(("group", "seq"), None, "tensor", None),
            P(None, ("group", "seq"), None),
            P(),
            P(),
        ),
        out_specs=P(None, ("group", "seq"), "tensor"),
        check_vma=False,
    )
```
